32 devices in a mesh: parts: 2 (over y), replica: 8 (over z, x), tensor: 2 (over core).
Axes of the slice: x: 2, y: 2, z: 4, core: 2. Of those that a mesh axis runs over, the one named last changes fastest.
Arguments:
- tokens: bfloat16 [2048, 8192], P(('parts', 'replica'), 'tensor'), parts along dimension 0, may hold values from -6 to 6
- base_output: bfloat16 [2048, 8192], P(('parts', 'replica'), 'tensor'), parts along dimension 0, may hold values from -6 to 6
- row_adapter_index: int32 [2048, 1], P(('parts', 'replica')), parts along dimension 0, may hold values from 0 to 7; in each aligned block of 128 rows (0 to 127, 128 to 255, ...) at most 32 rows name the same one
- adapter_table_index: int32 [8], replicated, may hold values from 0 to 7, each once
- adapter_down_table: bfloat16 [8, 8192, 64], P('replica', 'tensor'), may hold values from -0.0625 to 0.0625
- adapter_up_table: bfloat16 [8, 64, 8192], P('replica', None, 'tensor'), may hold values from -0.75 to 0.75
Outputs:
- adapted: bfloat16 [2048, 8192], P(('parts', 'replica'), 'tensor'), parts along dimension 0
The draws below stay inside these ranges and needn't reach their ends.
There are 2 independent parts, one for each index of `parts`. The reference program is written for one: setup_inputs(seed, part) draws one part's arguments, and reference() takes and returns one part's arrays. A program takes and returns all parts, laid end to end along the dimension named above; an argument that names none is the same for every part. Nothing has to cross between parts.
Inputs may be any that keep to these rules, and one draw needn't show every extreme that they name: `row_adapter_index`: within the rows of one replica, at most 32 rows name one adapter; some adapter is named by exactly 32 rows of some replica. `adapter_table_index`: each adapter has its own table index.
All inputs are finite; a program needn't handle non-finite values.
Results may differ from the reference program's by a relative error of at most 0.0056.
Values may be sent and summed in bfloat16 or wider, within the bound.
A program may use at most 64 MiB of HBM per device.

```python
import math
import jax
import jax.numpy as jnp
import numpy as np
from jax import lax

MODEL_WIDTH = 8192
ADAPTER_RANK = 64
ROWS = 128
ADAPTER_TOTAL = 8
CAP = 32
ROWS_ALL = 1024


def shard_levels(key, dims, split, smallest, largest):
    factor_of = 1.0
    for dim, blocks in split:
        heights = jax.random.uniform(jax.random.fold_in(jax.random.fold_in(key, 6), dim), (blocks,), jnp.float32, smallest / len(split), largest / len(split))
        factor_of = factor_of * jnp.repeat(jnp.exp(heights), dims[dim] // blocks).reshape((-1,) + (1,) * (len(dims) - 1 - dim))
    return factor_of


def shared_out(key, own, number, rows, count, top, most, skew):
    order = jax.random.permutation(key, count)
    crowded, usual = shares(count, rows * top, most, skew, True), shares(count, rows * top, most, skew, False)
    places = jnp.arange(count)

    def named(lengths, rotation):
        used = int((lengths > 0).sum())
        fixed = max(1, used // 4)
        moved = fixed + (places - fixed + rotation * (used - fixed)) % max(1, count - fixed)
        return jnp.zeros((count,), jnp.int32).at[order[jnp.where(places < fixed, places, moved)]].set(jnp.asarray(lengths, jnp.int32))

    lengths = jnp.where(number % 4 == 0, named(crowded, number // 4), named(usual, number - number // 4 - 1))
    mixed = jax.random.permutation(jax.random.fold_in(own, 3), count)
    donor, sink = mixed[0:count // 2 * 2:2], mixed[1:count // 2 * 2:2]
    room = jnp.minimum(lengths[donor] - 1, most - lengths[sink]) // 2
    room = jnp.where((donor == order[0]) | (sink == order[0]) | (lengths[sink] == 0), 0, jnp.maximum(room, 0))
    moved = jax.random.randint(jax.random.fold_in(own, 4), (count // 2,), 0, 1 << 20) % (room + 1)
    lengths = lengths.at[donor].add(-moved).at[sink].add(moved)
    items = jnp.searchsorted(jnp.cumsum(lengths), jnp.arange(rows * top), side="right").astype(jnp.int32)
    listing = items.reshape(top, rows).T
    listing = listing[jax.random.permutation(jax.random.fold_in(own, 1), rows)]
    rotation = jax.random.randint(jax.random.fold_in(own, 2), (rows, 1), 0, top)
    return jnp.take_along_axis(listing, (jnp.arange(top)[None, :] + rotation) % top, axis=1)


def shares(count, total, most, lean, full):
    portions = [(1 << 20) // math.isqrt(grade ** lean) + 1 for grade in range(1, count + 1)]
    largest = most if full else min(most, max(-(-total // count), total * portions[0] // sum(portions)))
    least = 1 if total - largest >= count - 1 else 0
    holding, rest = [largest] + [least] * (count - 1), total - largest - least * (count - 1)
    while rest > 0:
        candidates = [i for i in range(1, count) if holding[i] < largest] or [i for i in range(1, count) if holding[i] < most]
        pool, left = sum([portions[i] for i in candidates]), rest
        for i in candidates:
            extra = min(most - holding[i], max(1, left * portions[i] // pool), rest)
            holding[i] = holding[i] + extra
            rest = rest - extra
    return np.array(holding)


def gaussian(rng, extent, spread, reach, shards=(), kind=jnp.bfloat16):
    level = shard_levels(rng, extent, shards, -0.22, 0.18) if shards else 1.0
    entries = jax.random.normal(rng, extent, jnp.float32) * spread * level
    return jnp.minimum(jnp.maximum(entries, -reach), reach).astype(kind)


def setup_inputs(seed: int = 0, part: int = 0) -> dict:
    streams_of = jax.random.split(jax.random.key(seed), 7)
    part_splits = jax.random.split(jax.random.fold_in(streams_of[6], part), 7)
    tokens = gaussian(part_splits[0], (ROWS_ALL, MODEL_WIDTH), 1.0, 6.0, ((0, 8), (1, 2)))
    base_output = gaussian(part_splits[1], (ROWS_ALL, MODEL_WIDTH), 1.0, 6.0, ((0, 8), (1, 2)))
    row_adapter_index_keys = jax.random.split(jax.random.fold_in(part_splits[2], 1), ROWS_ALL // ROWS)
    row_adapter_index_turns = jax.random.permutation(jax.random.fold_in(part_splits[2], 3), ROWS_ALL // ROWS)
    row_adapter_index = jax.vmap(lambda own, number: shared_out(jax.random.fold_in(part_splits[2], 2), own, number, ROWS, ADAPTER_TOTAL, 1, CAP, 2))(row_adapter_index_keys, row_adapter_index_turns).reshape((ROWS_ALL, 1))
    adapter_table_index = jax.random.permutation(streams_of[3], ADAPTER_TOTAL).astype(jnp.int32)
    adapter_down_table = gaussian(streams_of[4], (ADAPTER_TOTAL, MODEL_WIDTH, ADAPTER_RANK), MODEL_WIDTH ** -0.5, 0.0625, ((0, 8), (1, 2)))
    adapter_up_table = gaussian(streams_of[5], (ADAPTER_TOTAL, ADAPTER_RANK, MODEL_WIDTH), ADAPTER_RANK ** -0.5, 0.75, ((0, 8), (2, 2)))
    return {"tokens": tokens, "base_output": base_output, "row_adapter_index": row_adapter_index, "adapter_table_index": adapter_table_index, "adapter_down_table": adapter_down_table, "adapter_up_table": adapter_up_table}


adapter_scale = 2.0


def reference(tokens, base_output, row_adapter_index, adapter_table_index, adapter_down_table, adapter_up_table):
    position = adapter_table_index[row_adapter_index[:, 0]].astype(jnp.int32)
    block_count = tokens.shape[0] // 16

    def one_block(index):
        start = (index * 16).astype(jnp.int32)
        pieces = lax.dynamic_slice_in_dim(tokens, start, 16, 0).astype(jnp.float32)
        matching_rows = lax.dynamic_slice_in_dim(position, start, 16, 0)
        down_weights = adapter_down_table[matching_rows].astype(jnp.float32)
        up_weights = adapter_up_table[matching_rows].astype(jnp.float32)
        reduced_activation = jnp.einsum("nd,ndr->nr", pieces, down_weights, precision=lax.Precision.HIGHEST).astype(jnp.bfloat16)
        delta = jnp.einsum("nr,nrd->nd", reduced_activation.astype(jnp.float32), up_weights, precision=lax.Precision.HIGHEST)
        return delta.astype(jnp.bfloat16)

    adapter_updates = lax.map(one_block, jnp.arange(block_count, dtype=jnp.int32))
    adapter_updates = adapter_updates.reshape(tokens.shape)
    return (base_output.astype(jnp.float32) + adapter_scale * adapter_updates.astype(jnp.float32)).astype(jnp.bfloat16)
```

```python
import functools

import jax
import jax.numpy as jnp
from jax import lax
from jax.experimental import pallas as pl
from jax.experimental.pallas import tpu as pltpu
from jax.sharding import PartitionSpec as P

adapter_scale = 2.0
MESH = pl.DeviceIdType.MESH
COLUMN_CHUNKS = 4


def row_exchange(
    tokens,
    base_output,
    row_adapter_index,
    adapter_table_index,
    adapter_down_table,
    adapter_up_table,
):
    replicas = lax.axis_size("replica")
    row_count = tokens.shape[0]
    kept_adapter_count = adapter_down_table.shape[0]
    total_adapters = adapter_table_index.shape[0]
    capacity = 2 * row_count // total_adapters
    row_ids = row_adapter_index[:, 0]
    numbers = jnp.arange(total_adapters, dtype=jnp.int32)
    position = jnp.sum(
        jnp.where(row_ids[:, None] == numbers[None, :], adapter_table_index[None, :], 0), axis=1
    )
    owner_rank = position // kept_adapter_count
    local_index = position % kept_adapter_count
    same_adapter = row_ids[:, None] == row_ids[None, :]
    row_numbers = jnp.arange(row_count, dtype=jnp.int32)
    earlier = row_numbers[None, :] < row_numbers[:, None]
    arrival = jnp.sum(jnp.logical_and(same_adapter, earlier).astype(jnp.int32), axis=1)
    destination = (
        owner_rank * (capacity * kept_adapter_count) + arrival * kept_adapter_count + local_index
    )
    slot_count = replicas * capacity * kept_adapter_count
    placing = (destination[None, :] == jnp.arange(slot_count, dtype=jnp.int32)[:, None]).astype(
        jnp.bfloat16
    )
    placing = placing.reshape(replicas, capacity, kept_adapter_count, row_count)
    outgoing = jnp.einsum(
        "scjn,nd->scjd", placing, tokens, preferred_element_type=jnp.float32
    ).astype(jnp.bfloat16)
    partial_value = jnp.einsum(
        "scjd,jdr->scjr",
        lax.all_to_all(outgoing, "replica", split_axis=0, concat_axis=0, tiled=True),
        adapter_down_table,
        preferred_element_type=jnp.float32,
    )
    reduced_activation = lax.psum(partial_value, "tensor").astype(jnp.bfloat16)
    served = jnp.einsum(
        "mqvn,vno->mqvo", reduced_activation, adapter_up_table, preferred_element_type=jnp.float32
    ).astype(jnp.bfloat16)
    returned = lax.all_to_all(served, "replica", split_axis=0, concat_axis=0, tiled=True)
    update_rows = jnp.einsum("scjn,scjd->nd", placing, returned, preferred_element_type=jnp.float32)
    return (base_output.astype(jnp.float32) + adapter_scale * update_rows).astype(jnp.bfloat16)


def flip(value, bit):
    return 1 - value if bit else value


def table_kernel(
    depth,
    ids_ref,
    table_ref,
    tok,
    wd,
    wu,
    out,
    xs,
    pos,
    down,
    up,
    dots,
    low_part,
    rs_src,
    rs_dst,
    ag,
    low,
    expanded,
    delta,
    local_sem,
    x_send,
    x_recv,
    pos_send,
    pos_recv,
    dx_send,
    ux_send,
    dz_send,
    uz_send,
    d_recv,
    u_recv,
    rs_send,
    rs_recv,
    ag_send,
    ag_recv,
    back_send,
    back_recv,
):
    rows = tok.shape[0]
    half = rows // 2
    quarter = tok.shape[1] // 4
    chunks, adapters, rank, width = up.shape
    lanes = 2 * rank
    part = lax.axis_index("parts")
    replica = lax.axis_index("replica")
    core = lax.axis_index("tensor")
    level, side = replica // 2, replica % 2
    beside = 2 * level + 1 - side

    def peer(e, other=0):
        return (flip(part, e >> 1), 2 * level + flip(side, e & 1), flip(core, other))

    def columns(e, offset=0, size=quarter):
        number = 2 * flip(part, e >> 1) + flip(side, e & 1)
        return pl.ds(pl.multiple_of(number * quarter + offset, 128), size)

    def remote(src, dst, send, recv, device):
        return pltpu.make_async_remote_copy(
            src_ref=src,
            dst_ref=dst,
            send_sem=send,
            recv_sem=recv,
            device_id=device,
            device_id_type=MESH,
        )

    def along(way):
        return (part, replica + (2 if way else -2), core)

    def can_go(way):
        return level < depth - 1 if way else level > 0

    def down_z(way, block, own=False):
        src = wd.at[:, columns(0)] if own else down.at[block]
        return remote(
            src, down.at[block], dz_send.at[way, block], d_recv.at[block], along(way)
        )

    def up_z(way, c, block, own=False):
        src = wu.at[:, columns(0, c * width, width)] if own else up.at[c, block]
        return remote(
            src,
            up.at[c, block],
            uz_send.at[way, c, block],
            u_recv.at[c, block],
            along(way),
        )

    def down_x():
        return remote(wd.at[:, columns(1)], down.at[replica], dx_send.at[0], d_recv.at[replica], peer(1))

    def up_x(c):
        return remote(
            wu.at[:, columns(1, c * width, width)],
            up.at[c, replica],
            ux_send.at[c],
            u_recv.at[c, replica],
            peer(1),
        )

    def wait_down(block):
        remote(down.at[block], down.at[block], dx_send.at[0], d_recv.at[block], peer(1)).wait_recv()

    def wait_up(c, block):
        remote(
            up.at[c, block], up.at[c, block], ux_send.at[c], u_recv.at[c, block], peer(1)
        ).wait_recv()

    def token_copy(e):
        return remote(tok.at[:, columns(e)], xs.at[e], x_send.at[e], x_recv.at[e], peer(e))

    def position_copy(e):
        return remote(pos.at[0], pos.at[e], pos_send.at[e], pos_recv.at[e], peer(e))

    def scatter_copy(d):
        return remote(
            rs_src.at[d], rs_dst.at[d], rs_send.at[d], rs_recv.at[d], peer(d >> 1, d & 1)
        )

    def gather_copy(d):
        return remote(ag.at[0], ag.at[d], ag_send.at[d], ag_recv.at[d], peer(d >> 1, d & 1))

    def back_copy(c, e):
        return remote(
            delta.at[c, e],
            out.at[:, columns(0, c * width, width)],
            back_send.at[c, e],
            back_recv.at[c, e],
            peer(e),
        )

    def back_wait(c, e):
        remote(
            delta.at[c, e],
            out.at[:, columns(e, c * width, width)],
            back_send.at[c, e],
            back_recv.at[c, e],
            peer(e),
        ).wait_recv()

    barrier = pltpu.get_barrier_semaphore()
    for d in range(1, 8):
        pl.semaphore_signal(barrier, inc=1, device_id=peer(d >> 1, d & 1), device_id_type=MESH)
    for way in (0, 1):

        @pl.when(can_go(way))
        def _():
            pl.semaphore_signal(barrier, inc=1, device_id=along(way), device_id_type=MESH)

    own_copies = [
        pltpu.make_async_copy(wd.at[:, columns(0)], down.at[replica], local_sem.at[0]),
        pltpu.make_async_copy(tok.at[:, columns(0)], xs.at[0], local_sem.at[1]),
    ] + [
        pltpu.make_async_copy(
            wu.at[:, columns(0, c * width, width)], up.at[c, replica], local_sem.at[2 + c]
        )
        for c in range(chunks)
    ]
    for copy in own_copies:
        copy.start()
    ids = ids_ref[...]
    position = jnp.zeros_like(ids)
    for a in range(adapters):
        position = jnp.where(ids == a, table_ref[a], position)
    pos[0] = jnp.broadcast_to(position.astype(jnp.float32), (8, rows))

    inner = jnp.logical_and(level > 0, level < depth - 1)
    pl.semaphore_wait(barrier, 8 + inner.astype(jnp.int32))

    down_x().start()
    for way in (0, 1):

        @pl.when(can_go(way))
        def _():
            down_z(way, replica, own=True).start()

    for c in range(chunks):
        up_x(c).start()
    for e in (1, 2, 3):
        position_copy(e).start()
    for e in (3, 1, 2):
        token_copy(e).start()
    wait_down(beside)
    for way in (0, 1):

        @pl.when(can_go(way))
        def _():
            down_z(way, beside).start()

    def start_own_up():
        for c in range(chunks):
            wait_up(c, beside)
            for way in (0, 1):

                @pl.when(can_go(way))
                def _():
                    up_z(way, c, replica, own=True).start()
                    up_z(way, c, beside).start()

    def arriving(step, wait, forward):
        for way in (0, 1):
            source = level - step if way else level + step

            @pl.when(source >= 0 if way else source < depth)
            def _():
                for block in (2 * source + side, 2 * source + 1 - side):
                    wait(block)

                    @pl.when(can_go(way))
                    def _():
                        forward(way, block).start()

    pl.when(jnp.logical_not(inner))(start_own_up)
    for step in range(1, depth):
        arriving(step, wait_down, down_z)
    pl.when(inner)(start_own_up)

    for copy in own_copies:
        copy.wait()
    for e in (1, 2, 3):
        position_copy(e).wait_recv()
        token_copy(e).wait_recv()
    dots[...] = lax.dot_general(
        xs[...].reshape(4 * rows, quarter),
        down[...].reshape(adapters * rank, quarter),
        (((1,), (1,)), ((), ())),
        preferred_element_type=jnp.float32,
    )
    upper = lax.broadcasted_iota(jnp.int32, (rows, lanes), 1) >= rank
    first = jnp.logical_not(upper)[: half // 2]

    def place_of(e):
        place = jnp.transpose(jnp.broadcast_to(pos[e][0:1], (lanes, rows)))
        return place.astype(jnp.int32) - upper.astype(jnp.int32)

    for e in range(4):
        place = place_of(e)
        total = jnp.zeros((rows, lanes), jnp.float32)
        for g in range(adapters // 2):
            part_dots = dots[e * rows : (e + 1) * rows, g * lanes : (g + 1) * lanes]
            total += jnp.where(place == 2 * g, part_dots, 0.0)
        low_part[e] = total + pltpu.roll(total, rank, 1)

    for d in range(8):
        start = pl.multiple_of(flip(core, d & 1) * half, half)
        rs_src[d] = jnp.where(
            first,
            low_part[d >> 1, pl.ds(start, half // 2)],
            low_part[d >> 1, pl.ds(start + half // 2, half // 2)],
        )
        if d:
            scatter_copy(d).start()
    summed = rs_src[0]
    for d in range(1, 8):
        scatter_copy(d).wait_recv()
        summed += rs_dst[d]
    ag[0] = summed.astype(jnp.bfloat16)
    for d in range(1, 8):
        gather_copy(d).start()
    for d in range(8):
        if d:
            gather_copy(d).wait_recv()
        packed = ag[d].astype(jnp.float32)
        rolled = pltpu.roll(packed, rank, 1)
        start = pl.multiple_of(flip(core, d & 1) * half, half)
        low[d >> 1, pl.ds(start, half // 2)] = jnp.where(first, packed, rolled)
        low[d >> 1, pl.ds(start + half // 2, half // 2)] = jnp.where(first, rolled, packed)
    for e in range(4):
        place = place_of(e)
        for g in range(adapters // 2):
            expanded[e * rows : (e + 1) * rows, g * lanes : (g + 1) * lanes] = jnp.where(
                place == 2 * g, low[e], 0.0
            ).astype(jnp.bfloat16)

    for c in range(chunks):
        for step in range(1, depth):
            arriving(step, functools.partial(wait_up, c), lambda way, b: up_z(way, c, b))
        product = jnp.dot(
            expanded[...],
            up[c].reshape(adapters * rank, width),
            preferred_element_type=jnp.float32,
        ).astype(jnp.bfloat16)
        delta[c] = product.reshape(4, rows, width)
        for e in (3, 1, 2):
            back_copy(c, e).start()
        pltpu.make_async_copy(
            delta.at[c, 0], out.at[:, columns(0, c * width, width)], local_sem.at[2 + c]
        ).start()

    for c in range(chunks):
        pltpu.make_async_copy(
            delta.at[c, 0], out.at[:, columns(0, c * width, width)], local_sem.at[2 + c]
        ).wait()
        for e in (1, 2, 3):
            back_wait(c, e)
            back_copy(c, e).wait_send()
    down_x().wait_send()
    for c in range(chunks):
        up_x(c).wait_send()
    for e in (1, 2, 3):
        position_copy(e).wait_send()
        token_copy(e).wait_send()
    for d in range(1, 8):
        scatter_copy(d).wait_send()
        gather_copy(d).wait_send()
    for way in (0, 1):
        for step in range(depth):
            source = level - step if way else level + step
            inside = source >= 0 if way else source < depth

            @pl.when(jnp.logical_and(inside, can_go(way)))
            def _():
                for block in (2 * source, 2 * source + 1):
                    down_z(way, block).wait_send()
                    for c in range(chunks):
                        up_z(way, c, block).wait_send()


def table_gather(
    tokens,
    base_output,
    row_adapter_index,
    adapter_table_index,
    adapter_down_table,
    adapter_up_table,
):
    rows, columns = tokens.shape
    adapters = adapter_table_index.shape[0]
    rank = adapter_up_table.shape[1]
    depth = adapters // 2
    quarter = columns // 4
    chunks = COLUMN_CHUNKS
    width = quarter // chunks
    lanes = 2 * rank
    half = rows // 2
    bf16, f32 = jnp.bfloat16, jnp.float32
    dma = pltpu.SemaphoreType.DMA
    anywhere = pl.BlockSpec(memory_space=pl.ANY)
    delta = pl.pallas_call(
        functools.partial(table_kernel, depth),
        out_shape=jax.ShapeDtypeStruct((rows, columns), bf16),
        in_specs=[
            pl.BlockSpec(memory_space=pltpu.VMEM),
            pl.BlockSpec(memory_space=pltpu.SMEM),
            anywhere,
            anywhere,
            anywhere,
        ],
        out_specs=anywhere,
        scratch_shapes=[
            pltpu.VMEM((4, rows, quarter), bf16),
            pltpu.VMEM((4, 8, rows), f32),
            pltpu.VMEM((adapters, rank, quarter), bf16),
            pltpu.VMEM((chunks, adapters, rank, width), bf16),
            pltpu.VMEM((4 * rows, adapters * rank), f32),
            pltpu.VMEM((4, rows, lanes), f32),
            pltpu.VMEM((8, half // 2, lanes), f32),
            pltpu.VMEM((8, half // 2, lanes), f32),
            pltpu.VMEM((8, half // 2, lanes), bf16),
            pltpu.VMEM((4, rows, lanes), f32),
            pltpu.VMEM((4 * rows, adapters * rank), bf16),
            pltpu.VMEM((chunks, 4, rows, width), bf16),
            dma((2 + chunks,)),
            dma((4,)),
            dma((4,)),
            dma((4,)),
            dma((4,)),
            dma((1,)),
            dma((chunks,)),
            dma((2, adapters)),
            dma((2, chunks, adapters)),
            dma((adapters,)),
            dma((chunks, adapters)),
            dma((8,)),
            dma((8,)),
            dma((8,)),
            dma((8,)),
            dma((chunks, 4)),
            dma((chunks, 4)),
        ],
        compiler_params=pltpu.CompilerParams(
            collective_id=0, has_side_effects=True, vmem_limit_bytes=40 * 1024 * 1024
        ),
    )(
        row_adapter_index.reshape(1, rows),
        adapter_table_index,
        tokens,
        adapter_down_table[0].T,
        adapter_up_table[0],
    )
    return (
        base_output.astype(jnp.float32) + adapter_scale * delta.astype(jnp.float32)
    ).astype(jnp.bfloat16)


def per_device(
    tokens,
    base_output,
    row_adapter_index,
    adapter_table_index,
    adapter_down_table,
    adapter_up_table,
):
    replicas = lax.axis_size("replica")
    rows, columns = tokens.shape
    kept, _, rank = adapter_down_table.shape
    tables = 2 * replicas * kept * rank * columns // 4
    slots = 2 * (2 * rows) * columns
    planes = (
        lax.axis_size("parts") == 2
        and lax.axis_size("tensor") == 2
        and replicas % 2 == 0
        and kept == 1
        and rows == 128
        and rank == 64
        and columns % (4 * COLUMN_CHUNKS * 128) == 0
    )
    plan = table_gather if planes and tables <= slots else row_exchange
    return plan(
        tokens,
        base_output,
        row_adapter_index,
        adapter_table_index,
        adapter_down_table,
        adapter_up_table,
    )


def solution(mesh):
    placed = (
        P(("parts", "replica"), "tensor"),
        P(("parts", "replica"), "tensor"),
        P(("parts", "replica"), None),
        P(),
        P("replica", "tensor", None),
        P("replica", None, "tensor"),
    )
    return jax.shard_map(
        per_device,
        mesh=mesh,
        in_specs=placed,
        out_specs=P(("parts", "replica"), "tensor"),
        check_vma=False,
    )
```

```python
import functools

import jax
import jax.numpy as jnp
from jax import lax
from jax.experimental import pallas as pl
from jax.experimental.pallas import tpu as pltpu
from jax.sharding import PartitionSpec as P

adapter_scale = 2.0
MESH = pl.DeviceIdType.MESH
CHUNK_EIGHTHS = (3, 3, 2)


def row_exchange(
    tokens,
    base_output,
    row_adapter_index,
    adapter_table_index,
    adapter_down_table,
    adapter_up_table,
):
    replicas = lax.axis_size("replica")
    row_count = tokens.shape[0]
    kept_adapter_count = adapter_down_table.shape[0]
    total_adapters = adapter_table_index.shape[0]
    capacity = 2 * row_count // total_adapters
    row_ids = row_adapter_index[:, 0]
    numbers = jnp.arange(total_adapters, dtype=jnp.int32)
    position = jnp.sum(
        jnp.where(row_ids[:, None] == numbers[None, :], adapter_table_index[None, :], 0), axis=1
    )
    owner_rank = position // kept_adapter_count
    local_index = position % kept_adapter_count
    same_adapter = row_ids[:, None] == row_ids[None, :]
    row_numbers = jnp.arange(row_count, dtype=jnp.int32)
    earlier = row_numbers[None, :] < row_numbers[:, None]
    arrival = jnp.sum(jnp.logical_and(same_adapter, earlier).astype(jnp.int32), axis=1)
    destination = (
        owner_rank * (capacity * kept_adapter_count) + arrival * kept_adapter_count + local_index
    )
    slot_count = replicas * capacity * kept_adapter_count
    placing = (destination[None, :] == jnp.arange(slot_count, dtype=jnp.int32)[:, None]).astype(
        jnp.bfloat16
    )
    placing = placing.reshape(replicas, capacity, kept_adapter_count, row_count)
    outgoing = jnp.einsum(
        "scjn,nd->scjd", placing, tokens, preferred_element_type=jnp.float32
    ).astype(jnp.bfloat16)
    partial_value = jnp.einsum(
        "scjd,jdr->scjr",
        lax.all_to_all(outgoing, "replica", split_axis=0, concat_axis=0, tiled=True),
        adapter_down_table,
        preferred_element_type=jnp.float32,
    )
    reduced_activation = lax.psum(partial_value, "tensor").astype(jnp.bfloat16)
    served = jnp.einsum(
        "mqvn,vno->mqvo", reduced_activation, adapter_up_table, preferred_element_type=jnp.float32
    ).astype(jnp.bfloat16)
    returned = lax.all_to_all(served, "replica", split_axis=0, concat_axis=0, tiled=True)
    update_rows = jnp.einsum("scjn,scjd->nd", placing, returned, preferred_element_type=jnp.float32)
    return (base_output.astype(jnp.float32) + adapter_scale * update_rows).astype(jnp.bfloat16)


def flip(value, bit):
    return 1 - value if bit else value


def table_kernel(
    depth,
    widths,
    ids_ref,
    table_ref,
    tok,
    wd,
    wu,
    out,
    xs,
    pos,
    down,
    dots,
    rs_src,
    rs_dst,
    ag,
    low,
    expanded,
    local_sem,
    x_send,
    x_recv,
    pos_send,
    pos_recv,
    dx_send,
    ux_send,
    ux_recv,
    dz_send,
    d_recv,
    uz_send,
    u_recv,
    rs_send,
    rs_recv,
    ag_send,
    ag_recv,
    back_send,
    back_recv,
    *buffers,
):
    chunks = len(widths)
    starts = [sum(widths[:c]) for c in range(chunks)]
    up, delta = buffers[:chunks], buffers[chunks:]
    rows = tok.shape[0]
    half = rows // 2
    quarter = tok.shape[1] // 4
    adapters, rank, _ = down.shape
    lanes = 2 * rank
    part = lax.axis_index("parts")
    replica = lax.axis_index("replica")
    core = lax.axis_index("tensor")
    level, side = replica // 2, replica % 2
    beside = 2 * level + 1 - side

    def peer(e, other=0):
        return (flip(part, e >> 1), 2 * level + flip(side, e & 1), flip(core, other))

    def columns(e, offset=0, size=quarter):
        number = 2 * flip(part, e >> 1) + flip(side, e & 1)
        return pl.ds(pl.multiple_of(number * quarter + offset, 128), size)

    def chunk(e, c):
        return columns(e, starts[c], widths[c])

    def pair(source):
        return pl.ds(2 * source, 2)

    def remote(src, dst, send, recv, device):
        return pltpu.make_async_remote_copy(
            src_ref=src,
            dst_ref=dst,
            send_sem=send,
            recv_sem=recv,
            device_id=device,
            device_id_type=MESH,
        )

    def along(way):
        return (part, replica + (2 if way else -2), core)

    def can_go(way):
        return level < depth - 1 if way else level > 0

    def down_z(way, block, own=False):
        src = wd.at[:, columns(0)] if own else down.at[block]
        return remote(src, down.at[block], dz_send.at[way, block], d_recv.at[block], along(way))

    def up_z(way, c, source):
        both = up[c].at[pair(source)]
        return remote(both, both, uz_send.at[way, c, source], u_recv.at[c, source], along(way))

    def down_x():
        return remote(
            wd.at[:, columns(1)], down.at[replica], dx_send.at[0], d_recv.at[replica], peer(1)
        )

    def up_x(c):
        return remote(
            wu.at[:, chunk(1, c)], up[c].at[replica], ux_send.at[c], ux_recv.at[c], peer(1)
        )

    def wait_down(block):
        there = down.at[block]
        remote(there, there, dx_send.at[0], d_recv.at[block], peer(1)).wait_recv()

    def wait_up(c, source):
        both = up[c].at[pair(source)]
        remote(both, both, ux_send.at[c], u_recv.at[c, source], peer(1)).wait_recv()

    def wait_up_x(c):
        there = up[c].at[beside]
        remote(there, there, ux_send.at[c], ux_recv.at[c], peer(1)).wait_recv()

    def token_copy(e):
        return remote(tok.at[:, columns(e)], xs.at[e], x_send.at[e], x_recv.at[e], peer(e))

    def position_copy(e):
        return remote(pos.at[0], pos.at[e], pos_send.at[e], pos_recv.at[e], peer(e))

    def scatter_copy(e, other):
        d = 2 * e + other
        src = rs_src.at[e, flip(core, other)]
        return remote(src, rs_dst.at[d], rs_send.at[d], rs_recv.at[d], peer(e, other))

    def gather_copy(d):
        return remote(ag.at[0], ag.at[d], ag_send.at[d], ag_recv.at[d], peer(d >> 1, d & 1))

    def back_copy(c, e):
        return remote(
            delta[c].at[e], out.at[:, chunk(0, c)], back_send.at[c, e], back_recv.at[c, e], peer(e)
        )

    def back_wait(c, e):
        remote(
            delta[c].at[e], out.at[:, chunk(e, c)], back_send.at[c, e], back_recv.at[c, e], peer(e)
        ).wait_recv()

    def own_back(c):
        return pltpu.make_async_copy(delta[c].at[0], out.at[:, chunk(0, c)], local_sem.at[2 + c])

    barrier = pltpu.get_barrier_semaphore()
    for d in range(1, 8):
        pl.semaphore_signal(barrier, inc=1, device_id=peer(d >> 1, d & 1), device_id_type=MESH)
    for way in (0, 1):

        @pl.when(can_go(way))
        def _():
            pl.semaphore_signal(barrier, inc=1, device_id=along(way), device_id_type=MESH)

    own_up = [
        pltpu.make_async_copy(wu.at[:, chunk(0, c)], up[c].at[replica], local_sem.at[2 + c])
        for c in range(chunks)
    ]
    own_down = [
        pltpu.make_async_copy(wd.at[:, columns(0)], down.at[replica], local_sem.at[0]),
        pltpu.make_async_copy(tok.at[:, columns(0)], xs.at[0], local_sem.at[1]),
    ]
    for copy in own_up + own_down:
        copy.start()
    ids = ids_ref[...]
    position = jnp.zeros_like(ids)
    for a in range(adapters):
        position = jnp.where(ids == a, table_ref[a], position)
    pos[0] = jnp.broadcast_to(position.astype(jnp.float32), (8, rows))

    inner = jnp.logical_and(level > 0, level < depth - 1)
    pl.semaphore_wait(barrier, 8 + inner.astype(jnp.int32))

    down_x().start()
    for way in (0, 1):

        @pl.when(can_go(way))
        def _():
            down_z(way, replica, own=True).start()

    for e in (3, 1, 2):
        token_copy(e).start()
    for e in (1, 2, 3):
        position_copy(e).start()
    for c in range(chunks):
        up_x(c).start()
    wait_down(beside)
    for way in (0, 1):

        @pl.when(can_go(way))
        def _():
            down_z(way, beside).start()

    for copy in own_up:
        copy.wait()

    def start_own_up():
        for c in range(chunks):
            wait_up_x(c)
            for way in (0, 1):

                @pl.when(can_go(way))
                def _():
                    up_z(way, c, level).start()

    def arriving(step, wait, forward):
        for way in (0, 1):
            source = level - step if way else level + step

            @pl.when(source >= 0 if way else source < depth)
            def _():
                wait(source)

                @pl.when(can_go(way))
                def _():
                    forward(way, source).start()

    def arriving_up(c, steps=range(1, depth)):
        for step in steps:
            arriving(step, functools.partial(wait_up, c), lambda way, s: up_z(way, c, s))

    pl.when(jnp.logical_not(inner))(start_own_up)
    for step in range(1, depth):
        for toward in (side, 1 - side):
            arriving(
                step,
                lambda source: wait_down(2 * source + toward),
                lambda way, source: down_z(way, 2 * source + toward),
            )
    pl.when(inner)(start_own_up)

    for copy in own_down:
        copy.wait()
    for e in (1, 2, 3):
        position_copy(e).wait_recv()
        token_copy(e).wait_recv()
    dots[...] = lax.dot_general(
        xs[...].reshape(4 * rows, quarter),
        down[...].reshape(adapters * rank, quarter),
        (((1,), (1,)), ((), ())),
        preferred_element_type=jnp.float32,
    )
    upper = lax.broadcasted_iota(jnp.int32, (rows, lanes), 1) >= rank
    first = jnp.logical_not(upper)[: half // 2]

    def place_of(e):
        place = jnp.transpose(jnp.broadcast_to(pos[e][0:1], (lanes, rows)))
        return place.astype(jnp.int32) - upper.astype(jnp.int32)

    for e in (3, 1, 2, 0):
        place = place_of(e)
        total = jnp.zeros((rows, lanes), jnp.float32)
        for g in range(adapters // 2):
            part_dots = dots[e * rows : (e + 1) * rows, g * lanes : (g + 1) * lanes]
            total += jnp.where(place == 2 * g, part_dots, 0.0)
        total += pltpu.roll(total, rank, 1)
        for h in (0, 1):
            lower = total[h * half : h * half + half // 2]
            higher = total[h * half + half // 2 : (h + 1) * half]
            rs_src[e, h] = jnp.where(first, lower, higher)
        for other in (1, 0):
            if e or other:
                scatter_copy(e, other).start()

    @pl.when(inner)
    def _():
        arriving_up(0, (1,))

    summed = rs_src[0, core]
    for d in range(1, 8):
        scatter_copy(d >> 1, d & 1).wait_recv()
        summed += rs_dst[d]
    ag[0] = summed.astype(jnp.bfloat16)
    for d in (7, 6, 3, 2, 5, 4, 1):
        gather_copy(d).start()

    @pl.when(inner)
    def _():
        arriving_up(0, range(2, depth))

    for d in range(8):
        if d:
            gather_copy(d).wait_recv()
        packed = ag[d].astype(jnp.float32)
        rolled = pltpu.roll(packed, rank, 1)
        start = pl.multiple_of(flip(core, d & 1) * half, half)
        low[d >> 1, pl.ds(start, half // 2)] = jnp.where(first, packed, rolled)
        low[d >> 1, pl.ds(start + half // 2, half // 2)] = jnp.where(first, rolled, packed)
    for e in range(4):
        place = place_of(e)
        for g in range(adapters // 2):
            expanded[e * rows : (e + 1) * rows, g * lanes : (g + 1) * lanes] = jnp.where(
                place == 2 * g, low[e], 0.0
            ).astype(jnp.bfloat16)

    for c in range(chunks):
        if c:
            arriving_up(c)
        else:
            pl.when(jnp.logical_not(inner))(functools.partial(arriving_up, c))
        product = jnp.dot(
            expanded[...],
            up[c][...].reshape(adapters * rank, widths[c]),
            preferred_element_type=jnp.float32,
        ).astype(jnp.bfloat16)
        delta[c][...] = product.reshape(4, rows, widths[c])
        for e in (3, 1, 2):
            back_copy(c, e).start()
        own_back(c).start()

    down_x().wait_send()
    for d in range(1, 8):
        scatter_copy(d >> 1, d & 1).wait_send()
        gather_copy(d).wait_send()
    for c in range(chunks):
        up_x(c).wait_send()
    for e in (1, 2, 3):
        position_copy(e).wait_send()
        token_copy(e).wait_send()
    for way in (0, 1):
        for step in range(depth):
            source = level - step if way else level + step
            inside = source >= 0 if way else source < depth

            @pl.when(jnp.logical_and(inside, can_go(way)))
            def _():
                down_z(way, 2 * source).wait_send()
                down_z(way, 2 * source + 1).wait_send()
                for c in range(chunks):
                    up_z(way, c, source).wait_send()

    for c in range(chunks):
        own_back(c).wait()
        for e in (1, 2, 3):
            back_wait(c, e)
            back_copy(c, e).wait_send()


def table_gather(
    tokens,
    base_output,
    row_adapter_index,
    adapter_table_index,
    adapter_down_table,
    adapter_up_table,
):
    rows, columns = tokens.shape
    adapters = adapter_table_index.shape[0]
    rank = adapter_up_table.shape[1]
    depth = adapters // 2
    quarter = columns // 4
    widths = tuple(quarter * share // 8 for share in CHUNK_EIGHTHS)
    chunks = len(widths)
    lanes = 2 * rank
    half = rows // 2
    bf16, f32 = jnp.bfloat16, jnp.float32
    dma = pltpu.SemaphoreType.DMA
    anywhere = pl.BlockSpec(memory_space=pl.ANY)
    delta = pl.pallas_call(
        functools.partial(table_kernel, depth, widths),
        out_shape=jax.ShapeDtypeStruct((rows, columns), bf16),
        in_specs=[
            pl.BlockSpec(memory_space=pltpu.VMEM),
            pl.BlockSpec(memory_space=pltpu.SMEM),
            anywhere,
            anywhere,
            anywhere,
        ],
        out_specs=anywhere,
        scratch_shapes=[
            pltpu.VMEM((4, rows, quarter), bf16),
            pltpu.VMEM((4, 8, rows), f32),
            pltpu.VMEM((adapters, rank, quarter), bf16),
            pltpu.VMEM((4 * rows, adapters * rank), f32),
            pltpu.VMEM((4, 2, half // 2, lanes), f32),
            pltpu.VMEM((8, half // 2, lanes), f32),
            pltpu.VMEM((8, half // 2, lanes), bf16),
            pltpu.VMEM((4, rows, lanes), f32),
            pltpu.VMEM((4 * rows, adapters * rank), bf16),
            dma((2 + chunks,)),
            dma((4,)),
            dma((4,)),
            dma((4,)),
            dma((4,)),
            dma((1,)),
            dma((chunks,)),
            dma((chunks,)),
            dma((2, adapters)),
            dma((adapters,)),
            dma((2, chunks, depth)),
            dma((chunks, depth)),
            dma((8,)),
            dma((8,)),
            dma((8,)),
            dma((8,)),
            dma((chunks, 4)),
            dma((chunks, 4)),
            *[pltpu.VMEM((adapters, rank, width), bf16) for width in widths],
            *[pltpu.VMEM((4, rows, width), bf16) for width in widths],
        ],
        compiler_params=pltpu.CompilerParams(
            collective_id=0, has_side_effects=True, vmem_limit_bytes=60 * 1024 * 1024
        ),
    )(
        row_adapter_index.reshape(1, rows),
        adapter_table_index,
        tokens,
        adapter_down_table[0].T,
        adapter_up_table[0],
    )
    return (
        base_output.astype(jnp.float32) + adapter_scale * delta.astype(jnp.float32)
    ).astype(jnp.bfloat16)


def per_device(
    tokens,
    base_output,
    row_adapter_index,
    adapter_table_index,
    adapter_down_table,
    adapter_up_table,
):
    replicas = lax.axis_size("replica")
    rows, columns = tokens.shape
    kept, _, rank = adapter_down_table.shape
    tables = 2 * replicas * kept * rank * columns // 4
    slots = 2 * (2 * rows) * columns
    planes = (
        lax.axis_size("parts") == 2
        and lax.axis_size("tensor") == 2
        and replicas % 2 == 0
        and kept == 1
        and rows == 128
        and rank == 64
        and columns % (4 * 8 * 128) == 0
    )
    plan = table_gather if planes and tables <= slots else row_exchange
    return plan(
        tokens,
        base_output,
        row_adapter_index,
        adapter_table_index,
        adapter_down_table,
        adapter_up_table,
    )


def solution(mesh):
    placed = (
        P(("parts", "replica"), "tensor"),
        P(("parts", "replica"), "tensor"),
        P(("parts", "replica"), None),
        P(),
        P("replica", "tensor", None),
        P("replica", None, "tensor"),
    )
    return jax.shard_map(
        per_device,
        mesh=mesh,
        in_specs=placed,
        out_specs=P(("parts", "replica"), "tensor"),
        check_vma=False,
    )
```

```python
import functools

import jax
import jax.numpy as jnp
from jax import lax
from jax.experimental import pallas as pl
from jax.experimental.pallas import tpu as pltpu
from jax.sharding import PartitionSpec as P

adapter_scale = 2.0
MESH = pl.DeviceIdType.MESH
CHUNK_EIGHTHS = (3, 2, 2, 1)


def row_exchange(
    tokens,
    base_output,
    row_adapter_index,
    adapter_table_index,
    adapter_down_table,
    adapter_up_table,
):
    replicas = lax.axis_size("replica")
    row_count = tokens.shape[0]
    kept_adapter_count = adapter_down_table.shape[0]
    total_adapters = adapter_table_index.shape[0]
    capacity = 2 * row_count // total_adapters
    row_ids = row_adapter_index[:, 0]
    numbers = jnp.arange(total_adapters, dtype=jnp.int32)
    position = jnp.sum(
        jnp.where(row_ids[:, None] == numbers[None, :], adapter_table_index[None, :], 0), axis=1
    )
    owner_rank = position // kept_adapter_count
    local_index = position % kept_adapter_count
    same_adapter = row_ids[:, None] == row_ids[None, :]
    row_numbers = jnp.arange(row_count, dtype=jnp.int32)
    earlier = row_numbers[None, :] < row_numbers[:, None]
    arrival = jnp.sum(jnp.logical_and(same_adapter, earlier).astype(jnp.int32), axis=1)
    destination = (
        owner_rank * (capacity * kept_adapter_count) + arrival * kept_adapter_count + local_index
    )
    slot_count = replicas * capacity * kept_adapter_count
    placing = (destination[None, :] == jnp.arange(slot_count, dtype=jnp.int32)[:, None]).astype(
        jnp.bfloat16
    )
    placing = placing.reshape(replicas, capacity, kept_adapter_count, row_count)
    outgoing = jnp.einsum(
        "scjn,nd->scjd", placing, tokens, preferred_element_type=jnp.float32
    ).astype(jnp.bfloat16)
    partial_value = jnp.einsum(
        "scjd,jdr->scjr",
        lax.all_to_all(outgoing, "replica", split_axis=0, concat_axis=0, tiled=True),
        adapter_down_table,
        preferred_element_type=jnp.float32,
    )
    reduced_activation = lax.psum(partial_value, "tensor").astype(jnp.bfloat16)
    served = jnp.einsum(
        "mqvn,vno->mqvo", reduced_activation, adapter_up_table, preferred_element_type=jnp.float32
    ).astype(jnp.bfloat16)
    returned = lax.all_to_all(served, "replica", split_axis=0, concat_axis=0, tiled=True)
    update_rows = jnp.einsum("scjn,scjd->nd", placing, returned, preferred_element_type=jnp.float32)
    return (base_output.astype(jnp.float32) + adapter_scale * update_rows).astype(jnp.bfloat16)


def flip(value, bit):
    return 1 - value if bit else value


def table_kernel(
    depth,
    widths,
    ids_hbm,
    table_hbm,
    tok,
    wd,
    wu,
    out,
    xs,
    pos,
    down,
    dots,
    rs_src,
    rs_dst,
    ag,
    low,
    expanded,
    local_sem,
    x_send,
    x_recv,
    pos_send,
    pos_recv,
    dx_send,
    ux_send,
    ux_recv,
    dz_send,
    d_recv,
    uz_send,
    u_recv,
    rs_send,
    rs_recv,
    ag_send,
    ag_recv,
    back_send,
    back_recv,
    ids_ref,
    table_ref,
    *buffers,
):
    chunks = len(widths)
    starts = [sum(widths[:c]) for c in range(chunks)]
    up, delta = buffers[:chunks], buffers[chunks:]
    rows = tok.shape[0]
    half = rows // 2
    quarter = tok.shape[1] // 4
    adapters, rank, _ = down.shape
    lanes = 2 * rank
    part = lax.axis_index("parts")
    replica = lax.axis_index("replica")
    core = lax.axis_index("tensor")
    level, side = replica // 2, replica % 2
    beside = 2 * level + 1 - side

    def peer(e, other=0):
        return (flip(part, e >> 1), 2 * level + flip(side, e & 1), flip(core, other))

    def columns(e, offset=0, size=quarter):
        number = 2 * flip(part, e >> 1) + flip(side, e & 1)
        return pl.ds(pl.multiple_of(number * quarter + offset, 128), size)

    def chunk(e, c):
        return columns(e, starts[c], widths[c])

    def pair(source):
        return pl.ds(2 * source, 2)

    def remote(src, dst, send, recv, device):
        return pltpu.make_async_remote_copy(
            src_ref=src,
            dst_ref=dst,
            send_sem=send,
            recv_sem=recv,
            device_id=device,
            device_id_type=MESH,
        )

    def along(way):
        return (part, replica + (2 if way else -2), core)

    def can_go(way):
        return level < depth - 1 if way else level > 0

    def down_z(way, block, own=False):
        src = wd.at[:, columns(0)] if own else down.at[block]
        return remote(src, down.at[block], dz_send.at[way, block], d_recv.at[block], along(way))

    def up_z(way, c, source):
        both = up[c].at[pair(source)]
        return remote(both, both, uz_send.at[way, c, source], u_recv.at[c, source], along(way))

    def down_x():
        return remote(
            wd.at[:, columns(1)], down.at[replica], dx_send.at[0], d_recv.at[replica], peer(1)
        )

    def up_x(c):
        return remote(
            wu.at[:, chunk(1, c)], up[c].at[replica], ux_send.at[c], ux_recv.at[c], peer(1)
        )

    def wait_down(block):
        there = down.at[block]
        remote(there, there, dx_send.at[0], d_recv.at[block], peer(1)).wait_recv()

    def wait_up(c, source):
        both = up[c].at[pair(source)]
        remote(both, both, ux_send.at[c], u_recv.at[c, source], peer(1)).wait_recv()

    def wait_up_x(c):
        there = up[c].at[beside]
        remote(there, there, ux_send.at[c], ux_recv.at[c], peer(1)).wait_recv()

    def token_copy(e):
        return remote(tok.at[:, columns(e)], xs.at[e], x_send.at[e], x_recv.at[e], peer(e))

    def position_copy(e):
        return remote(pos.at[0], pos.at[e], pos_send.at[e], pos_recv.at[e], peer(e))

    def scatter_copy(e, other):
        d = 2 * e + other
        src = rs_src.at[e, flip(core, other)]
        return remote(src, rs_dst.at[d], rs_send.at[d], rs_recv.at[d], peer(e, other))

    def gather_copy(d):
        return remote(ag.at[0], ag.at[d], ag_send.at[d], ag_recv.at[d], peer(d >> 1, d & 1))

    def back_copy(c, e):
        return remote(
            delta[c].at[e], out.at[:, chunk(0, c)], back_send.at[c, e], back_recv.at[c, e], peer(e)
        )

    def back_wait(c, e):
        remote(
            delta[c].at[e], out.at[:, chunk(e, c)], back_send.at[c, e], back_recv.at[c, e], peer(e)
        ).wait_recv()

    def own_back(c):
        return pltpu.make_async_copy(delta[c].at[0], out.at[:, chunk(0, c)], local_sem.at[2 + c])

    barrier = pltpu.get_barrier_semaphore()
    for d in range(1, 8):
        pl.semaphore_signal(barrier, inc=1, device_id=peer(d >> 1, d & 1), device_id_type=MESH)
    for way in (0, 1):

        @pl.when(can_go(way))
        def _():
            pl.semaphore_signal(barrier, inc=1, device_id=along(way), device_id_type=MESH)

    own_up = [
        pltpu.make_async_copy(wu.at[:, chunk(0, c)], up[c].at[replica], local_sem.at[2 + c])
        for c in range(chunks)
    ]
    own_down = [
        pltpu.make_async_copy(wd.at[:, columns(0)], down.at[replica], local_sem.at[0]),
        pltpu.make_async_copy(tok.at[:, columns(0)], xs.at[0], local_sem.at[1]),
    ]
    indices = [
        pltpu.make_async_copy(ids_hbm, ids_ref, local_sem.at[2 + chunks]),
        pltpu.make_async_copy(table_hbm, table_ref, local_sem.at[3 + chunks]),
    ]
    for copy in indices + own_up + own_down:
        copy.start()
    for copy in indices:
        copy.wait()
    ids = ids_ref[...]
    position = jnp.zeros_like(ids)
    for a in range(adapters):
        position = jnp.where(ids == a, table_ref[a], position)
    pos[0] = jnp.broadcast_to(position.astype(jnp.float32), (8, rows))

    inner = jnp.logical_and(level > 0, level < depth - 1)
    pl.semaphore_wait(barrier, 8 + inner.astype(jnp.int32))

    down_x().start()
    for way in (0, 1):

        @pl.when(can_go(way))
        def _():
            down_z(way, replica, own=True).start()

    for e in (3, 1, 2):
        token_copy(e).start()
    for e in (1, 2, 3):
        position_copy(e).start()
    for c in range(chunks):
        up_x(c).start()
    wait_down(beside)
    for way in (0, 1):

        @pl.when(can_go(way))
        def _():
            down_z(way, beside).start()

    for copy in own_up:
        copy.wait()

    def start_own_up(numbers):
        for c in numbers:
            wait_up_x(c)
            for way in (0, 1):

                @pl.when(can_go(way))
                def _():
                    up_z(way, c, level).start()

    def arriving(step, wait, forward):
        for way in (0, 1):
            source = level - step if way else level + step

            @pl.when(source >= 0 if way else source < depth)
            def _():
                wait(source)

                @pl.when(can_go(way))
                def _():
                    forward(way, source).start()

    def arriving_up(c, steps=range(1, depth)):
        for step in steps:
            arriving(step, functools.partial(wait_up, c), lambda way, s: up_z(way, c, s))

    def pass_ahead(c):
        if c < chunks:
            arriving_up(c, range(2, depth))
        if c + 1 < chunks:
            arriving_up(c + 1, (1,))

    pl.when(jnp.logical_not(inner))(functools.partial(start_own_up, range(chunks)))
    for step in range(1, depth):
        for toward in (side, 1 - side):
            arriving(
                step,
                lambda source: wait_down(2 * source + toward),
                lambda way, source: down_z(way, 2 * source + toward),
            )
    pl.when(inner)(functools.partial(start_own_up, (0,)))

    for copy in own_down:
        copy.wait()
    for e in (1, 2, 3):
        position_copy(e).wait_recv()
        token_copy(e).wait_recv()
    dots[...] = lax.dot_general(
        xs[...].reshape(4 * rows, quarter),
        down[...].reshape(adapters * rank, quarter),
        (((1,), (1,)), ((), ())),
        preferred_element_type=jnp.float32,
    )
    upper = lax.broadcasted_iota(jnp.int32, (rows, lanes), 1) >= rank
    first = jnp.logical_not(upper)[: half // 2]

    def place_of(e):
        place = jnp.transpose(jnp.broadcast_to(pos[e][0:1], (lanes, rows)))
        return place.astype(jnp.int32) - upper.astype(jnp.int32)

    for e in (3, 1, 2, 0):
        place = place_of(e)
        total = jnp.zeros((rows, lanes), jnp.float32)
        for g in range(adapters // 2):
            part_dots = dots[e * rows : (e + 1) * rows, g * lanes : (g + 1) * lanes]
            total += jnp.where(place == 2 * g, part_dots, 0.0)
        total += pltpu.roll(total, rank, 1)
        for h in (0, 1):
            lower = total[h * half : h * half + half // 2]
            higher = total[h * half + half // 2 : (h + 1) * half]
            rs_src[e, h] = jnp.where(first, lower, higher)
        for other in (1, 0):
            if e or other:
                scatter_copy(e, other).start()

    @pl.when(inner)
    def _():
        arriving_up(0, (1,))
        start_own_up(range(1, chunks))

    summed = rs_src[0, core]
    for d in range(1, 8):
        scatter_copy(d >> 1, d & 1).wait_recv()
        summed += rs_dst[d]
    ag[0] = summed.astype(jnp.bfloat16)
    for d in (7, 6, 3, 2, 5, 4, 1):
        gather_copy(d).start()

    pl.when(inner)(functools.partial(pass_ahead, 0))

    for d in range(8):
        if d:
            gather_copy(d).wait_recv()
        packed = ag[d].astype(jnp.float32)
        rolled = pltpu.roll(packed, rank, 1)
        start = pl.multiple_of(flip(core, d & 1) * half, half)
        low[d >> 1, pl.ds(start, half // 2)] = jnp.where(first, packed, rolled)
        low[d >> 1, pl.ds(start + half // 2, half // 2)] = jnp.where(first, rolled, packed)
    for e in range(4):
        place = place_of(e)
        for g in range(adapters // 2):
            expanded[e * rows : (e + 1) * rows, g * lanes : (g + 1) * lanes] = jnp.where(
                place == 2 * g, low[e], 0.0
            ).astype(jnp.bfloat16)

    for c in range(chunks):
        pl.when(jnp.logical_not(inner))(functools.partial(arriving_up, c))
        pl.when(inner)(functools.partial(pass_ahead, c + 1))
        product = jnp.dot(
            expanded[...],
            up[c][...].reshape(adapters * rank, widths[c]),
            preferred_element_type=jnp.float32,
        ).astype(jnp.bfloat16)
        delta[c][...] = product.reshape(4, rows, widths[c])
        for e in (3, 1, 2):
            back_copy(c, e).start()
        own_back(c).start()

    down_x().wait_send()
    for d in range(1, 8):
        scatter_copy(d >> 1, d & 1).wait_send()
        gather_copy(d).wait_send()
    for c in range(chunks):
        up_x(c).wait_send()
    for e in (1, 2, 3):
        position_copy(e).wait_send()
        token_copy(e).wait_send()
    for way in (0, 1):
        for step in range(depth):
            source = level - step if way else level + step
            inside = source >= 0 if way else source < depth

            @pl.when(jnp.logical_and(inside, can_go(way)))
            def _():
                down_z(way, 2 * source).wait_send()
                down_z(way, 2 * source + 1).wait_send()
                for c in range(chunks):
                    up_z(way, c, source).wait_send()

    for c in range(chunks):
        own_back(c).wait()
        for e in (1, 2, 3):
            back_wait(c, e)
            back_copy(c, e).wait_send()


def table_gather(
    tokens,
    base_output,
    row_adapter_index,
    adapter_table_index,
    adapter_down_table,
    adapter_up_table,
):
    rows, columns = tokens.shape
    adapters = adapter_table_index.shape[0]
    rank = adapter_up_table.shape[1]
    depth = adapters // 2
    quarter = columns // 4
    widths = tuple(quarter * share // 8 for share in CHUNK_EIGHTHS)
    chunks = len(widths)
    lanes = 2 * rank
    half = rows // 2
    bf16, f32 = jnp.bfloat16, jnp.float32
    dma = pltpu.SemaphoreType.DMA
    anywhere = pl.BlockSpec(memory_space=pl.ANY)
    delta = pl.pallas_call(
        functools.partial(table_kernel, depth, widths),
        out_shape=jax.ShapeDtypeStruct((rows, columns), bf16),
        in_specs=[
            anywhere,
            anywhere,
            anywhere,
            anywhere,
            anywhere,
        ],
        out_specs=anywhere,
        scratch_shapes=[
            pltpu.VMEM((4, rows, quarter), bf16),
            pltpu.VMEM((4, 8, rows), f32),
            pltpu.VMEM((adapters, rank, quarter), bf16),
            pltpu.VMEM((4 * rows, adapters * rank), f32),
            pltpu.VMEM((4, 2, half // 2, lanes), f32),
            pltpu.VMEM((8, half // 2, lanes), f32),
            pltpu.VMEM((8, half // 2, lanes), bf16),
            pltpu.VMEM((4, rows, lanes), f32),
            pltpu.VMEM((4 * rows, adapters * rank), bf16),
            dma((4 + chunks,)),
            dma((4,)),
            dma((4,)),
            dma((4,)),
            dma((4,)),
            dma((1,)),
            dma((chunks,)),
            dma((chunks,)),
            dma((2, adapters)),
            dma((adapters,)),
            dma((2, chunks, depth)),
            dma((chunks, depth)),
            dma((8,)),
            dma((8,)),
            dma((8,)),
            dma((8,)),
            dma((chunks, 4)),
            dma((chunks, 4)),
            pltpu.VMEM((1, rows), jnp.int32),
            pltpu.SMEM((adapters,), jnp.int32),
            *[pltpu.VMEM((adapters, rank, width), bf16) for width in widths],
            *[pltpu.VMEM((4, rows, width), bf16) for width in widths],
        ],
        compiler_params=pltpu.CompilerParams(
            collective_id=0, has_side_effects=True, vmem_limit_bytes=40 * 1024 * 1024
        ),
    )(
        *[
            pltpu.with_memory_space_constraint(operand, pltpu.HBM)
            for operand in (
                row_adapter_index.reshape(1, rows),
                adapter_table_index,
                tokens,
                adapter_down_table[0].T,
                adapter_up_table[0],
            )
        ]
    )
    return (
        base_output.astype(jnp.float32) + adapter_scale * delta.astype(jnp.float32)
    ).astype(jnp.bfloat16)


def per_device(
    tokens,
    base_output,
    row_adapter_index,
    adapter_table_index,
    adapter_down_table,
    adapter_up_table,
):
    replicas = lax.axis_size("replica")
    rows, columns = tokens.shape
    kept, _, rank = adapter_down_table.shape
    tables = 2 * replicas * kept * rank * columns // 4
    slots = 2 * (2 * rows) * columns
    planes = (
        lax.axis_size("parts") == 2
        and lax.axis_size("tensor") == 2
        and replicas % 2 == 0
        and kept == 1
        and rows == 128
        and rank == 64
        and columns % (4 * 8 * 128) == 0
    )
    plan = table_gather if planes and tables <= slots else row_exchange
    return plan(
        tokens,
        base_output,
        row_adapter_index,
        adapter_table_index,
        adapter_down_table,
        adapter_up_table,
    )


def solution(mesh):
    placed = (
        P(("parts", "replica"), "tensor"),
        P(("parts", "replica"), "tensor"),
        P(("parts", "replica"), None),
        P(),
        P("replica", "tensor", None),
        P("replica", None, "tensor"),
    )
    return jax.shard_map(
        per_device,
        mesh=mesh,
        in_specs=placed,
        out_specs=P(("parts", "replica"), "tensor"),
        check_vma=False,
    )
```

```python
import functools

import jax
import jax.numpy as jnp
from jax import lax
from jax.experimental import pallas as pl
from jax.experimental.pallas import tpu as pltpu
from jax.sharding import PartitionSpec as P

adapter_scale = 2.0
MESH = pl.DeviceIdType.MESH
CHUNK_EIGHTHS = (3, 2, 2, 1)


def row_exchange(
    tokens,
    base_output,
    row_adapter_index,
    adapter_table_index,
    adapter_down_table,
    adapter_up_table,
):
    replicas = lax.axis_size("replica")
    row_count = tokens.shape[0]
    kept_adapter_count = adapter_down_table.shape[0]
    total_adapters = adapter_table_index.shape[0]
    capacity = 2 * row_count // total_adapters
    row_ids = row_adapter_index[:, 0]
    numbers = jnp.arange(total_adapters, dtype=jnp.int32)
    position = jnp.sum(
        jnp.where(row_ids[:, None] == numbers[None, :], adapter_table_index[None, :], 0), axis=1
    )
    owner_rank = position // kept_adapter_count
    local_index = position % kept_adapter_count
    same_adapter = row_ids[:, None] == row_ids[None, :]
    row_numbers = jnp.arange(row_count, dtype=jnp.int32)
    earlier = row_numbers[None, :] < row_numbers[:, None]
    arrival = jnp.sum(jnp.logical_and(same_adapter, earlier).astype(jnp.int32), axis=1)
    destination = (
        owner_rank * (capacity * kept_adapter_count) + arrival * kept_adapter_count + local_index
    )
    slot_count = replicas * capacity * kept_adapter_count
    placing = (destination[None, :] == jnp.arange(slot_count, dtype=jnp.int32)[:, None]).astype(
        jnp.bfloat16
    )
    placing = placing.reshape(replicas, capacity, kept_adapter_count, row_count)
    outgoing = jnp.einsum(
        "scjn,nd->scjd", placing, tokens, preferred_element_type=jnp.float32
    ).astype(jnp.bfloat16)
    partial_value = jnp.einsum(
        "scjd,jdr->scjr",
        lax.all_to_all(outgoing, "replica", split_axis=0, concat_axis=0, tiled=True),
        adapter_down_table,
        preferred_element_type=jnp.float32,
    )
    reduced_activation = lax.psum(partial_value, "tensor").astype(jnp.bfloat16)
    served = jnp.einsum(
        "mqvn,vno->mqvo", reduced_activation, adapter_up_table, preferred_element_type=jnp.float32
    ).astype(jnp.bfloat16)
    returned = lax.all_to_all(served, "replica", split_axis=0, concat_axis=0, tiled=True)
    update_rows = jnp.einsum("scjn,scjd->nd", placing, returned, preferred_element_type=jnp.float32)
    return (base_output.astype(jnp.float32) + adapter_scale * update_rows).astype(jnp.bfloat16)


def flip(value, bit):
    return 1 - value if bit else value


def table_kernel(
    depth,
    widths,
    ids_hbm,
    table_hbm,
    tok,
    wd,
    wu,
    out,
    xs,
    pos,
    down,
    dots,
    rs_src,
    rs_dst,
    ag,
    low,
    expanded,
    local_sem,
    x_send,
    x_recv,
    pos_send,
    pos_recv,
    dx_send,
    ux_send,
    ux_recv,
    dz_send,
    d_recv,
    uz_send,
    u_recv,
    rs_send,
    rs_recv,
    ag_send,
    ag_recv,
    back_send,
    back_recv,
    ids_ref,
    table_ref,
    place_of,
    *buffers,
):
    chunks = len(widths)
    starts = [sum(widths[:c]) for c in range(chunks)]
    up, delta = buffers[:chunks], buffers[chunks:]
    rows = tok.shape[0]
    half = rows // 2
    quarter = tok.shape[1] // 4
    adapters, rank, _ = down.shape
    lanes = 2 * rank
    part = lax.axis_index("parts")
    replica = lax.axis_index("replica")
    core = lax.axis_index("tensor")
    level, side = replica // 2, replica % 2
    beside = 2 * level + 1 - side

    def peer(e, other=0):
        return (flip(part, e >> 1), 2 * level + flip(side, e & 1), flip(core, other))

    def columns(e, offset=0, size=quarter):
        number = 2 * flip(part, e >> 1) + flip(side, e & 1)
        return pl.ds(pl.multiple_of(number * quarter + offset, 128), size)

    def chunk(e, c):
        return columns(e, starts[c], widths[c])

    def pair(source):
        return pl.ds(2 * source, 2)

    def remote(src, dst, send, recv, device):
        return pltpu.make_async_remote_copy(
            src_ref=src,
            dst_ref=dst,
            send_sem=send,
            recv_sem=recv,
            device_id=device,
            device_id_type=MESH,
        )

    def along(way):
        return (part, replica + (2 if way else -2), core)

    def can_go(way):
        return level < depth - 1 if way else level > 0

    def down_z(way, block, own=False):
        src = wd.at[:, columns(0)] if own else down.at[block]
        return remote(src, down.at[block], dz_send.at[way, block], d_recv.at[block], along(way))

    def up_z(way, c, source):
        both = up[c].at[pair(source)]
        return remote(both, both, uz_send.at[way, c, source], u_recv.at[c, source], along(way))

    def down_x():
        return remote(
            wd.at[:, columns(1)], down.at[replica], dx_send.at[0], d_recv.at[replica], peer(1)
        )

    def up_x(c):
        return remote(
            wu.at[:, chunk(1, c)], up[c].at[replica], ux_send.at[c], ux_recv.at[c], peer(1)
        )

    def wait_down(block):
        there = down.at[block]
        remote(there, there, dx_send.at[0], d_recv.at[block], peer(1)).wait_recv()

    def wait_up(c, source):
        both = up[c].at[pair(source)]
        remote(both, both, ux_send.at[c], u_recv.at[c, source], peer(1)).wait_recv()

    def wait_up_x(c):
        there = up[c].at[beside]
        remote(there, there, ux_send.at[c], ux_recv.at[c], peer(1)).wait_recv()

    def token_copy(e):
        return remote(tok.at[:, columns(e)], xs.at[e], x_send.at[e], x_recv.at[e], peer(e))

    def position_copy(e):
        return remote(pos.at[0], pos.at[e], pos_send.at[e], pos_recv.at[e], peer(e))

    def scatter_copy(e, other):
        d = 2 * e + other
        src = rs_src.at[e, flip(core, other)]
        return remote(src, rs_dst.at[d], rs_send.at[d], rs_recv.at[d], peer(e, other))

    def gather_copy(d):
        return remote(ag.at[0], ag.at[d], ag_send.at[d], ag_recv.at[d], peer(d >> 1, d & 1))

    def back_copy(c, e):
        return remote(
            delta[c].at[e], out.at[:, chunk(0, c)], back_send.at[c, e], back_recv.at[c, e], peer(e)
        )

    def back_wait(c, e):
        remote(
            delta[c].at[e], out.at[:, chunk(e, c)], back_send.at[c, e], back_recv.at[c, e], peer(e)
        ).wait_recv()

    def own_back(c):
        return pltpu.make_async_copy(delta[c].at[0], out.at[:, chunk(0, c)], local_sem.at[2 + c])

    barrier = pltpu.get_barrier_semaphore()
    for d in range(1, 8):
        pl.semaphore_signal(barrier, inc=1, device_id=peer(d >> 1, d & 1), device_id_type=MESH)
    for way in (0, 1):

        @pl.when(can_go(way))
        def _():
            pl.semaphore_signal(barrier, inc=1, device_id=along(way), device_id_type=MESH)

    own_up = [
        pltpu.make_async_copy(wu.at[:, chunk(0, c)], up[c].at[replica], local_sem.at[2 + c])
        for c in range(chunks)
    ]
    own_down = [
        pltpu.make_async_copy(wd.at[:, columns(0)], down.at[replica], local_sem.at[0]),
        pltpu.make_async_copy(tok.at[:, columns(0)], xs.at[0], local_sem.at[1]),
    ]
    indices = [
        pltpu.make_async_copy(ids_hbm, ids_ref, local_sem.at[2 + chunks]),
        pltpu.make_async_copy(table_hbm, table_ref, local_sem.at[3 + chunks]),
    ]
    for copy in indices + own_up + own_down:
        copy.start()
    for copy in indices:
        copy.wait()
    ids = ids_ref[...]
    position = jnp.zeros_like(ids)
    for a in range(adapters):
        position = jnp.where(ids == a, table_ref[a], position)
    pos[0] = jnp.broadcast_to(position.astype(jnp.float32), (8, rows))

    inner = jnp.logical_and(level > 0, level < depth - 1)
    pl.semaphore_wait(barrier, 8 + inner.astype(jnp.int32))

    down_x().start()
    for way in (0, 1):

        @pl.when(can_go(way))
        def _():
            down_z(way, replica, own=True).start()

    for e in (3, 1, 2):
        token_copy(e).start()
    for e in (1, 2, 3):
        position_copy(e).start()
    for c in range(chunks):
        up_x(c).start()
    wait_down(beside)
    for way in (0, 1):

        @pl.when(can_go(way))
        def _():
            down_z(way, beside).start()

    for copy in own_up:
        copy.wait()

    def start_own_up(numbers):
        for c in numbers:
            wait_up_x(c)
            for way in (0, 1):

                @pl.when(can_go(way))
                def _():
                    up_z(way, c, level).start()

    def arriving(step, wait, forward):
        for way in (0, 1):
            source = level - step if way else level + step

            @pl.when(source >= 0 if way else source < depth)
            def _():
                wait(source)

                @pl.when(can_go(way))
                def _():
                    forward(way, source).start()

    def arriving_up(c, steps=range(1, depth)):
        for step in steps:
            arriving(step, functools.partial(wait_up, c), lambda way, s: up_z(way, c, s))

    def pass_ahead(c):
        if c < chunks:
            arriving_up(c, range(2, depth))
        if c + 1 < chunks:
            arriving_up(c + 1, (1,))

    pl.when(jnp.logical_not(inner))(functools.partial(start_own_up, range(chunks)))
    def arriving_down(step):
        for toward in (side, 1 - side):
            arriving(
                step,
                lambda source: wait_down(2 * source + toward),
                lambda way, source: down_z(way, 2 * source + toward),
            )

    for step in range(1, depth - 1):
        arriving_down(step)
    pl.when(inner)(functools.partial(start_own_up, (0,)))

    upper = lax.broadcasted_iota(jnp.int32, (rows, lanes), 1) >= rank
    first = jnp.logical_not(upper)[: half // 2]
    for copy in own_down:
        copy.wait()
    for e in range(4):
        if e:
            position_copy(e).wait_recv()
        spread = jnp.transpose(jnp.broadcast_to(pos[e][0:1], (lanes, rows)))
        place_of[e] = spread.astype(jnp.int32) - upper.astype(jnp.int32)
    for e in (1, 2, 3):
        token_copy(e).wait_recv()
    arriving_down(depth - 1)

    dots[...] = lax.dot_general(
        xs[...].reshape(4 * rows, quarter),
        down[...].reshape(adapters * rank, quarter),
        (((1,), (1,)), ((), ())),
        preferred_element_type=jnp.float32,
    )
    for e in (3, 1, 2, 0):
        place = place_of[e]
        total = jnp.zeros((rows, lanes), jnp.float32)
        for g in range(adapters // 2):
            part_dots = dots[e * rows : (e + 1) * rows, g * lanes : (g + 1) * lanes]
            total += jnp.where(place == 2 * g, part_dots, 0.0)
        total += pltpu.roll(total, rank, 1)
        for h in (0, 1):
            lower = total[h * half : h * half + half // 2]
            higher = total[h * half + half // 2 : (h + 1) * half]
            rs_src[e, h] = jnp.where(first, lower, higher)
        for other in (1, 0):
            if e or other:
                scatter_copy(e, other).start()

    @pl.when(inner)
    def _():
        arriving_up(0, (1,))
        start_own_up(range(1, chunks))

    summed = rs_src[0, core]
    for d in range(1, 8):
        scatter_copy(d >> 1, d & 1).wait_recv()
        summed += rs_dst[d]
    ag[0] = summed.astype(jnp.bfloat16)
    for d in (7, 6, 3, 2, 5, 4, 1):
        gather_copy(d).start()

    pl.when(inner)(functools.partial(pass_ahead, 0))

    pl.when(jnp.logical_not(inner))(functools.partial(arriving_up, 0))
    for e in (3, 1, 2, 0):
        for d in (2 * e, 2 * e + 1):
            if d:
                gather_copy(d).wait_recv()
            packed = ag[d].astype(jnp.float32)
            rolled = pltpu.roll(packed, rank, 1)
            start = pl.multiple_of(flip(core, d & 1) * half, half)
            low[e, pl.ds(start, half // 2)] = jnp.where(first, packed, rolled)
            low[e, pl.ds(start + half // 2, half // 2)] = jnp.where(first, rolled, packed)
        place = place_of[e]
        for g in range(adapters // 2):
            expanded[e * rows : (e + 1) * rows, g * lanes : (g + 1) * lanes] = jnp.where(
                place == 2 * g, low[e], 0.0
            ).astype(jnp.bfloat16)
        delta[0][e] = jnp.dot(
            expanded[e * rows : (e + 1) * rows],
            up[0][...].reshape(adapters * rank, widths[0]),
            preferred_element_type=jnp.float32,
        ).astype(jnp.bfloat16)
        if e:
            back_copy(0, e).start()
    own_back(0).start()
    pl.when(inner)(functools.partial(pass_ahead, 1))

    for c in range(1, chunks):
        pl.when(jnp.logical_not(inner))(functools.partial(arriving_up, c))
        pl.when(inner)(functools.partial(pass_ahead, c + 1))
        product = jnp.dot(
            expanded[...],
            up[c][...].reshape(adapters * rank, widths[c]),
            preferred_element_type=jnp.float32,
        ).astype(jnp.bfloat16)
        delta[c][...] = product.reshape(4, rows, widths[c])
        for e in (3, 1, 2):
            back_copy(c, e).start()
        own_back(c).start()

    down_x().wait_send()
    for d in range(1, 8):
        scatter_copy(d >> 1, d & 1).wait_send()
        gather_copy(d).wait_send()
    for c in range(chunks):
        up_x(c).wait_send()
    for e in (1, 2, 3):
        position_copy(e).wait_send()
        token_copy(e).wait_send()
    for way in (0, 1):
        for step in range(depth):
            source = level - step if way else level + step
            inside = source >= 0 if way else source < depth

            @pl.when(jnp.logical_and(inside, can_go(way)))
            def _():
                down_z(way, 2 * source).wait_send()
                down_z(way, 2 * source + 1).wait_send()
                for c in range(chunks):
                    up_z(way, c, source).wait_send()

    for c in range(chunks):
        own_back(c).wait()
        for e in (1, 2, 3):
            back_wait(c, e)
            back_copy(c, e).wait_send()


def table_gather(
    tokens,
    base_output,
    row_adapter_index,
    adapter_table_index,
    adapter_down_table,
    adapter_up_table,
):
    rows, columns = tokens.shape
    adapters = adapter_table_index.shape[0]
    rank = adapter_up_table.shape[1]
    depth = adapters // 2
    quarter = columns // 4
    widths = tuple(quarter * share // 8 for share in CHUNK_EIGHTHS)
    chunks = len(widths)
    lanes = 2 * rank
    half = rows // 2
    bf16, f32 = jnp.bfloat16, jnp.float32
    dma = pltpu.SemaphoreType.DMA
    anywhere = pl.BlockSpec(memory_space=pl.ANY)
    delta = pl.pallas_call(
        functools.partial(table_kernel, depth, widths),
        out_shape=jax.ShapeDtypeStruct((rows, columns), bf16),
        in_specs=[
            anywhere,
            anywhere,
            anywhere,
            anywhere,
            anywhere,
        ],
        out_specs=anywhere,
        scratch_shapes=[
            pltpu.VMEM((4, rows, quarter), bf16),
            pltpu.VMEM((4, 8, rows), f32),
            pltpu.VMEM((adapters, rank, quarter), bf16),
            pltpu.VMEM((4 * rows, adapters * rank), f32),
            pltpu.VMEM((4, 2, half // 2, lanes), f32),
            pltpu.VMEM((8, half // 2, lanes), f32),
            pltpu.VMEM((8, half // 2, lanes), bf16),
            pltpu.VMEM((4, rows, lanes), f32),
            pltpu.VMEM((4 * rows, adapters * rank), bf16),
            dma((4 + chunks,)),
            dma((4,)),
            dma((4,)),
            dma((4,)),
            dma((4,)),
            dma((1,)),
            dma((chunks,)),
            dma((chunks,)),
            dma((2, adapters)),
            dma((adapters,)),
            dma((2, chunks, depth)),
            dma((chunks, depth)),
            dma((8,)),
            dma((8,)),
            dma((8,)),
            dma((8,)),
            dma((chunks, 4)),
            dma((chunks, 4)),
            pltpu.VMEM((1, rows), jnp.int32),
            pltpu.SMEM((adapters,), jnp.int32),
            pltpu.VMEM((4, rows, lanes), jnp.int32),
            *[pltpu.VMEM((adapters, rank, width), bf16) for width in widths],
            *[pltpu.VMEM((4, rows, width), bf16) for width in widths],
        ],
        compiler_params=pltpu.CompilerParams(
            collective_id=0, has_side_effects=True, vmem_limit_bytes=40 * 1024 * 1024
        ),
    )(
        *[
            pltpu.with_memory_space_constraint(operand, pltpu.HBM)
            for operand in (
                row_adapter_index.reshape(1, rows),
                adapter_table_index,
                tokens,
                adapter_down_table[0].T,
                adapter_up_table[0],
            )
        ]
    )
    return (
        base_output.astype(jnp.float32) + adapter_scale * delta.astype(jnp.float32)
    ).astype(jnp.bfloat16)


def per_device(
    tokens,
    base_output,
    row_adapter_index,
    adapter_table_index,
    adapter_down_table,
    adapter_up_table,
):
    replicas = lax.axis_size("replica")
    rows, columns = tokens.shape
    kept, _, rank = adapter_down_table.shape
    tables = 2 * replicas * kept * rank * columns // 4
    slots = 2 * (2 * rows) * columns
    planes = (
        lax.axis_size("parts") == 2
        and lax.axis_size("tensor") == 2
        and replicas % 2 == 0
        and kept == 1
        and rows == 128
        and rank == 64
        and columns % (4 * 8 * 128) == 0
    )
    plan = table_gather if planes and tables <= slots else row_exchange
    return plan(
        tokens,
        base_output,
        row_adapter_index,
        adapter_table_index,
        adapter_down_table,
        adapter_up_table,
    )


def solution(mesh):
    placed = (
        P(("parts", "replica"), "tensor"),
        P(("parts", "replica"), "tensor"),
        P(("parts", "replica"), None),
        P(),
        P("replica", "tensor", None),
        P("replica", None, "tensor"),
    )
    return jax.shard_map(
        per_device,
        mesh=mesh,
        in_specs=placed,
        out_specs=P(("parts", "replica"), "tensor"),
        check_vma=False,
    )
```

```python
import functools

import jax
import jax.numpy as jnp
from jax import lax
from jax.experimental import pallas as pl
from jax.experimental.pallas import tpu as pltpu
from jax.sharding import PartitionSpec as P

adapter_scale = 2.0
MESH = pl.DeviceIdType.MESH
CHUNK_EIGHTHS = (3, 2, 2, 1)


def row_exchange(
    tokens,
    base_output,
    row_adapter_index,
    adapter_table_index,
    adapter_down_table,
    adapter_up_table,
):
    replicas = lax.axis_size("replica")
    row_count = tokens.shape[0]
    kept_adapter_count = adapter_down_table.shape[0]
    total_adapters = adapter_table_index.shape[0]
    capacity = 2 * row_count // total_adapters
    row_ids = row_adapter_index[:, 0]
    numbers = jnp.arange(total_adapters, dtype=jnp.int32)
    position = jnp.sum(
        jnp.where(row_ids[:, None] == numbers[None, :], adapter_table_index[None, :], 0), axis=1
    )
    owner_rank = position // kept_adapter_count
    local_index = position % kept_adapter_count
    same_adapter = row_ids[:, None] == row_ids[None, :]
    row_numbers = jnp.arange(row_count, dtype=jnp.int32)
    earlier = row_numbers[None, :] < row_numbers[:, None]
    arrival = jnp.sum(jnp.logical_and(same_adapter, earlier).astype(jnp.int32), axis=1)
    destination = (
        owner_rank * (capacity * kept_adapter_count) + arrival * kept_adapter_count + local_index
    )
    slot_count = replicas * capacity * kept_adapter_count
    placing = (destination[None, :] == jnp.arange(slot_count, dtype=jnp.int32)[:, None]).astype(
        jnp.bfloat16
    )
    placing = placing.reshape(replicas, capacity, kept_adapter_count, row_count)
    outgoing = jnp.einsum(
        "scjn,nd->scjd", placing, tokens, preferred_element_type=jnp.float32
    ).astype(jnp.bfloat16)
    partial_value = jnp.einsum(
        "scjd,jdr->scjr",
        lax.all_to_all(outgoing, "replica", split_axis=0, concat_axis=0, tiled=True),
        adapter_down_table,
        preferred_element_type=jnp.float32,
    )
    reduced_activation = lax.psum(partial_value, "tensor").astype(jnp.bfloat16)
    served = jnp.einsum(
        "mqvn,vno->mqvo", reduced_activation, adapter_up_table, preferred_element_type=jnp.float32
    ).astype(jnp.bfloat16)
    returned = lax.all_to_all(served, "replica", split_axis=0, concat_axis=0, tiled=True)
    update_rows = jnp.einsum("scjn,scjd->nd", placing, returned, preferred_element_type=jnp.float32)
    return (base_output.astype(jnp.float32) + adapter_scale * update_rows).astype(jnp.bfloat16)


def flip(value, bit):
    return 1 - value if bit else value


def table_kernel(
    depth,
    widths,
    ids_hbm,
    table_hbm,
    tok,
    wd,
    wu,
    out,
    xs,
    pos,
    down,
    dots,
    rs_src,
    rs_dst,
    ag,
    low,
    expanded,
    local_sem,
    x_send,
    x_recv,
    pos_send,
    pos_recv,
    dx_send,
    ux_send,
    ux_recv,
    dz_send,
    d_recv,
    uz_send,
    u_recv,
    rs_send,
    rs_recv,
    ag_send,
    ag_recv,
    back_send,
    back_recv,
    ids_ref,
    table_ref,
    *buffers,
):
    chunks = len(widths)
    starts = [sum(widths[:c]) for c in range(chunks)]
    up, delta = buffers[:chunks], buffers[chunks:]
    rows = tok.shape[0]
    half = rows // 2
    quarter = tok.shape[1] // 4
    adapters, rank, _ = down.shape
    lanes = 2 * rank
    part = lax.axis_index("parts")
    replica = lax.axis_index("replica")
    core = lax.axis_index("tensor")
    level, side = replica // 2, replica % 2
    beside = 2 * level + 1 - side

    def peer(e, other=0):
        return (flip(part, e >> 1), 2 * level + flip(side, e & 1), flip(core, other))

    def columns(e, offset=0, size=quarter):
        number = 2 * flip(part, e >> 1) + flip(side, e & 1)
        return pl.ds(pl.multiple_of(number * quarter + offset, 128), size)

    def chunk(e, c):
        return columns(e, starts[c], widths[c])

    def pair(source):
        return pl.ds(2 * source, 2)

    def remote(src, dst, send, recv, device):
        return pltpu.make_async_remote_copy(
            src_ref=src,
            dst_ref=dst,
            send_sem=send,
            recv_sem=recv,
            device_id=device,
            device_id_type=MESH,
        )

    def along(way):
        return (part, replica + (2 if way else -2), core)

    def can_go(way):
        return level < depth - 1 if way else level > 0

    def down_z(way, block, own=False):
        src = wd.at[:, columns(0)] if own else down.at[block]
        return remote(src, down.at[block], dz_send.at[way, block], d_recv.at[block], along(way))

    def up_z(way, c, source):
        both = up[c].at[pair(source)]
        return remote(both, both, uz_send.at[way, c, source], u_recv.at[c, source], along(way))

    def down_x():
        return remote(
            wd.at[:, columns(1)], down.at[replica], dx_send.at[0], d_recv.at[replica], peer(1)
        )

    def up_x(c):
        return remote(
            wu.at[:, chunk(1, c)], up[c].at[replica], ux_send.at[c], ux_recv.at[c], peer(1)
        )

    def wait_down(block):
        there = down.at[block]
        remote(there, there, dx_send.at[0], d_recv.at[block], peer(1)).wait_recv()

    def wait_up(c, source):
        both = up[c].at[pair(source)]
        remote(both, both, ux_send.at[c], u_recv.at[c, source], peer(1)).wait_recv()

    def wait_up_x(c):
        there = up[c].at[beside]
        remote(there, there, ux_send.at[c], ux_recv.at[c], peer(1)).wait_recv()

    def token_copy(e):
        return remote(tok.at[:, columns(e)], xs.at[e], x_send.at[e], x_recv.at[e], peer(e))

    def position_copy(e):
        return remote(pos.at[0], pos.at[e], pos_send.at[e], pos_recv.at[e], peer(e))

    def scatter_copy(e, other):
        d = 2 * e + other
        src = rs_src.at[e, flip(core, other)]
        return remote(src, rs_dst.at[d], rs_send.at[d], rs_recv.at[d], peer(e, other))

    def gather_copy(d):
        return remote(ag.at[0], ag.at[d], ag_send.at[d], ag_recv.at[d], peer(d >> 1, d & 1))

    def back_copy(c, e):
        return remote(
            delta[c].at[e], out.at[:, chunk(0, c)], back_send.at[c, e], back_recv.at[c, e], peer(e)
        )

    def back_wait(c, e):
        remote(
            delta[c].at[e], out.at[:, chunk(e, c)], back_send.at[c, e], back_recv.at[c, e], peer(e)
        ).wait_recv()

    def own_back(c):
        return pltpu.make_async_copy(delta[c].at[0], out.at[:, chunk(0, c)], local_sem.at[2 + c])

    barrier = pltpu.get_barrier_semaphore()
    for d in range(1, 8):
        pl.semaphore_signal(barrier, inc=1, device_id=peer(d >> 1, d & 1), device_id_type=MESH)
    for way in (0, 1):

        @pl.when(can_go(way))
        def _():
            pl.semaphore_signal(barrier, inc=1, device_id=along(way), device_id_type=MESH)

    own_up = [
        pltpu.make_async_copy(wu.at[:, chunk(0, c)], up[c].at[replica], local_sem.at[2 + c])
        for c in range(chunks)
    ]
    own_down = [
        pltpu.make_async_copy(wd.at[:, columns(0)], down.at[replica], local_sem.at[0]),
        pltpu.make_async_copy(tok.at[:, columns(0)], xs.at[0], local_sem.at[1]),
    ]
    indices = [
        pltpu.make_async_copy(ids_hbm, ids_ref, local_sem.at[2 + chunks]),
        pltpu.make_async_copy(table_hbm, table_ref, local_sem.at[3 + chunks]),
    ]
    for copy in indices + own_up + own_down:
        copy.start()
    for copy in indices:
        copy.wait()
    ids = ids_ref[...]
    position = jnp.zeros_like(ids)
    for a in range(adapters):
        position = jnp.where(ids == a, table_ref[a], position)
    pos[0] = jnp.broadcast_to(position.astype(jnp.float32), (8, rows))

    inner = jnp.logical_and(level > 0, level < depth - 1)
    pl.semaphore_wait(barrier, 8 + inner.astype(jnp.int32))

    down_x().start()
    for way in (0, 1):

        @pl.when(can_go(way))
        def _():
            down_z(way, replica, own=True).start()

    def start_up_x():
        for c in range(chunks):
            up_x(c).start()

    pl.when(jnp.logical_not(inner))(start_up_x)
    for e in (3, 1, 2):
        token_copy(e).start()
    for e in (1, 2, 3):
        position_copy(e).start()
    pl.when(inner)(start_up_x)
    wait_down(beside)
    for way in (0, 1):

        @pl.when(can_go(way))
        def _():
            down_z(way, beside).start()

    for copy in own_up:
        copy.wait()

    def start_own_up(numbers):
        for c in numbers:
            wait_up_x(c)
            for way in (0, 1):

                @pl.when(can_go(way))
                def _():
                    up_z(way, c, level).start()

    def arriving(step, wait, forward):
        for way in (0, 1):
            source = level - step if way else level + step

            @pl.when(source >= 0 if way else source < depth)
            def _():
                wait(source)

                @pl.when(can_go(way))
                def _():
                    forward(way, source).start()

    def arriving_up(c, steps=range(1, depth)):
        for step in steps:
            arriving(step, functools.partial(wait_up, c), lambda way, s: up_z(way, c, s))

    def pass_ahead(c):
        if c < chunks:
            arriving_up(c, range(2, depth))
        if c + 1 < chunks:
            arriving_up(c + 1, (1,))

    pl.when(jnp.logical_not(inner))(functools.partial(start_own_up, range(chunks)))
    for step in range(1, depth):
        for toward in (side, 1 - side):
            arriving(
                step,
                lambda source: wait_down(2 * source + toward),
                lambda way, source: down_z(way, 2 * source + toward),
            )
    pl.when(inner)(functools.partial(start_own_up, (0,)))

    for copy in own_down:
        copy.wait()
    for e in (1, 2, 3):
        position_copy(e).wait_recv()
        token_copy(e).wait_recv()
    dots[...] = lax.dot_general(
        xs[...].reshape(4 * rows, quarter),
        down[...].reshape(adapters * rank, quarter),
        (((1,), (1,)), ((), ())),
        preferred_element_type=jnp.float32,
    )
    upper = lax.broadcasted_iota(jnp.int32, (rows, lanes), 1) >= rank
    first = jnp.logical_not(upper)[: half // 2]

    def place_of(e):
        place = jnp.transpose(jnp.broadcast_to(pos[e][0:1], (lanes, rows)))
        return place.astype(jnp.int32) - upper.astype(jnp.int32)

    for e in (3, 1, 2, 0):
        place = place_of(e)
        total = jnp.zeros((rows, lanes), jnp.float32)
        for g in range(adapters // 2):
            part_dots = dots[e * rows : (e + 1) * rows, g * lanes : (g + 1) * lanes]
            total += jnp.where(place == 2 * g, part_dots, 0.0)
        total += pltpu.roll(total, rank, 1)
        for h in (0, 1):
            lower = total[h * half : h * half + half // 2]
            higher = total[h * half + half // 2 : (h + 1) * half]
            rs_src[e, h] = jnp.where(first, lower, higher)
        for other in (1, 0):
            if e or other:
                scatter_copy(e, other).start()

    @pl.when(inner)
    def _():
        arriving_up(0, (1,))
        start_own_up(range(1, chunks))

    summed = rs_src[0, core]
    for d in range(1, 8):
        scatter_copy(d >> 1, d & 1).wait_recv()
        summed += rs_dst[d]
    ag[0] = summed.astype(jnp.bfloat16)
    for d in (7, 6, 3, 2, 5, 4, 1):
        gather_copy(d).start()

    pl.when(inner)(functools.partial(pass_ahead, 0))

    for d in range(8):
        if d:
            gather_copy(d).wait_recv()
        packed = ag[d].astype(jnp.float32)
        rolled = pltpu.roll(packed, rank, 1)
        start = pl.multiple_of(flip(core, d & 1) * half, half)
        low[d >> 1, pl.ds(start, half // 2)] = jnp.where(first, packed, rolled)
        low[d >> 1, pl.ds(start + half // 2, half // 2)] = jnp.where(first, rolled, packed)
    for e in range(4):
        place = place_of(e)
        for g in range(adapters // 2):
            expanded[e * rows : (e + 1) * rows, g * lanes : (g + 1) * lanes] = jnp.where(
                place == 2 * g, low[e], 0.0
            ).astype(jnp.bfloat16)

    for c in range(chunks):
        pl.when(jnp.logical_not(inner))(functools.partial(arriving_up, c))
        pl.when(inner)(functools.partial(pass_ahead, c + 1))
        product = jnp.dot(
            expanded[...],
            up[c][...].reshape(adapters * rank, widths[c]),
            preferred_element_type=jnp.float32,
        ).astype(jnp.bfloat16)
        delta[c][...] = product.reshape(4, rows, widths[c])
        for e in (3, 1, 2):
            back_copy(c, e).start()
        own_back(c).start()

    down_x().wait_send()
    for d in range(1, 8):
        scatter_copy(d >> 1, d & 1).wait_send()
        gather_copy(d).wait_send()
    for c in range(chunks):
        up_x(c).wait_send()
    for e in (1, 2, 3):
        position_copy(e).wait_send()
        token_copy(e).wait_send()
    for way in (0, 1):
        for step in range(depth):
            source = level - step if way else level + step
            inside = source >= 0 if way else source < depth

            @pl.when(jnp.logical_and(inside, can_go(way)))
            def _():
                down_z(way, 2 * source).wait_send()
                down_z(way, 2 * source + 1).wait_send()
                for c in range(chunks):
                    up_z(way, c, source).wait_send()

    for c in range(chunks):
        own_back(c).wait()
        for e in (1, 2, 3):
            back_wait(c, e)
            back_copy(c, e).wait_send()


def table_gather(
    tokens,
    base_output,
    row_adapter_index,
    adapter_table_index,
    adapter_down_table,
    adapter_up_table,
):
    rows, columns = tokens.shape
    adapters = adapter_table_index.shape[0]
    rank = adapter_up_table.shape[1]
    depth = adapters // 2
    quarter = columns // 4
    widths = tuple(quarter * share // 8 for share in CHUNK_EIGHTHS)
    chunks = len(widths)
    lanes = 2 * rank
    half = rows // 2
    bf16, f32 = jnp.bfloat16, jnp.float32
    dma = pltpu.SemaphoreType.DMA
    anywhere = pl.BlockSpec(memory_space=pl.ANY)
    delta = pl.pallas_call(
        functools.partial(table_kernel, depth, widths),
        out_shape=jax.ShapeDtypeStruct((rows, columns), bf16),
        in_specs=[
            anywhere,
            anywhere,
            anywhere,
            anywhere,
            anywhere,
        ],
        out_specs=anywhere,
        scratch_shapes=[
            pltpu.VMEM((4, rows, quarter), bf16),
            pltpu.VMEM((4, 8, rows), f32),
            pltpu.VMEM((adapters, rank, quarter), bf16),
            pltpu.VMEM((4 * rows, adapters * rank), f32),
            pltpu.VMEM((4, 2, half // 2, lanes), f32),
            pltpu.VMEM((8, half // 2, lanes), f32),
            pltpu.VMEM((8, half // 2, lanes), bf16),
            pltpu.VMEM((4, rows, lanes), f32),
            pltpu.VMEM((4 * rows, adapters * rank), bf16),
            dma((4 + chunks,)),
            dma((4,)),
            dma((4,)),
            dma((4,)),
            dma((4,)),
            dma((1,)),
            dma((chunks,)),
            dma((chunks,)),
            dma((2, adapters)),
            dma((adapters,)),
            dma((2, chunks, depth)),
            dma((chunks, depth)),
            dma((8,)),
            dma((8,)),
            dma((8,)),
            dma((8,)),
            dma((chunks, 4)),
            dma((chunks, 4)),
            pltpu.VMEM((1, rows), jnp.int32),
            pltpu.SMEM((adapters,), jnp.int32),
            *[pltpu.VMEM((adapters, rank, width), bf16) for width in widths],
            *[pltpu.VMEM((4, rows, width), bf16) for width in widths],
        ],
        compiler_params=pltpu.CompilerParams(
            collective_id=0, has_side_effects=True, vmem_limit_bytes=40 * 1024 * 1024
        ),
    )(
        *[
            pltpu.with_memory_space_constraint(operand, pltpu.HBM)
            for operand in (
                row_adapter_index.reshape(1, rows),
                adapter_table_index,
                tokens,
                adapter_down_table[0].T,
                adapter_up_table[0],
            )
        ]
    )
    return (
        base_output.astype(jnp.float32) + adapter_scale * delta.astype(jnp.float32)
    ).astype(jnp.bfloat16)


def per_device(
    tokens,
    base_output,
    row_adapter_index,
    adapter_table_index,
    adapter_down_table,
    adapter_up_table,
):
    replicas = lax.axis_size("replica")
    rows, columns = tokens.shape
    kept, _, rank = adapter_down_table.shape
    tables = 2 * replicas * kept * rank * columns // 4
    slots = 2 * (2 * rows) * columns
    planes = (
        lax.axis_size("parts") == 2
        and lax.axis_size("tensor") == 2
        and replicas % 2 == 0
        and kept == 1
        and rows == 128
        and rank == 64
        and columns % (4 * 8 * 128) == 0
    )
    plan = table_gather if planes and tables <= slots else row_exchange
    return plan(
        tokens,
        base_output,
        row_adapter_index,
        adapter_table_index,
        adapter_down_table,
        adapter_up_table,
    )


def solution(mesh):
    placed = (
        P(("parts", "replica"), "tensor"),
        P(("parts", "replica"), "tensor"),
        P(("parts", "replica"), None),
        P(),
        P("replica", "tensor", None),
        P("replica", None, "tensor"),
    )
    return jax.shard_map(
        per_device,
        mesh=mesh,
        in_specs=placed,
        out_specs=P(("parts", "replica"), "tensor"),
        check_vma=False,
    )
```
